512 devices in a mesh: section: 32 (over z, y_hi), tensor: 8 (over x, y_lo), dp: 2 (over core).
Axes of the slice: x: 4, y: 4 (y_hi: 2, y_lo: 2; y = y_hi * 2 + y_lo), z: 16, core: 2. Of those that a mesh axis runs over, the one named last changes fastest.
Arguments:
- start_acts: bfloat16 [32, 256, 5120], P('section', 'dp', 'tensor'), may hold values from -6 to 6
- fresh_acts: bfloat16 [2, 256, 5120], P(None, 'dp', 'tensor'), may hold values from -6 to 6
- ln_gain: float32 [32, 5120], P('section'), may hold values from 0.1 to 1.9
- ln_shift: float32 [32, 5120], P('section'), may hold values from -4 to 4
- proj: bfloat16 [32, 5120, 5120], P('section', 'dp', 'tensor'), may hold values from -0.078125 to 0.078125
- proj_bias: float32 [32, 5120], P('section', 'tensor'), may hold values from -6 to 6
- sample_ids: int32 [34, 4], P(None, 'dp'), may hold values from 0 to 3
- base_out: bfloat16 [32, 8, 64, 5120], P('section', 'dp', None, 'tensor'), may hold values from -6 to 6
- base_in: bfloat16 [32, 8, 64, 5120], P('section', 'dp', None, 'tensor'), may hold values from -6 to 6
- scale_exps: int32 [32, 3, 256, 40], P('section', None, 'dp', 'tensor'), may hold values from -1 to 2
Outputs:
- layer_out: bfloat16 [32, 3, 256, 5120], P('section', None, 'dp', 'tensor')
- last_arrived: bfloat16 [32, 256, 5120], P('section', 'dp', 'tensor')
The draws below stay inside these ranges and needn't reach their ends.
Inputs may be any that keep to these rules, and one draw needn't show every extreme that they name: `sample_ids`: each replica stores 4 samples; an id names a slot within its own replica's store.
All inputs are finite; a program needn't handle non-finite values.
Results may differ from the reference program's by a relative error of at most 0.012.
Values may be sent and summed in bfloat16 or wider, within the bound.
No kernel may reach another device: no remote copies, remote signals or barrier semaphores. Data moves between devices by JAX's collectives and lax.ppermute only.
A program may use at most 64 MiB of HBM per device.

```python
import jax
import jax.numpy as jnp
from jax import lax

D = 5120
BLOCK = 128
SEQLEN = 64
SEQS = 2
STORE = 4
TICKS = 3
ROWS = 128
SECTIONS = 32
MICRO = 34
NBLK = 40
N_DP = 2


def place_ends(entries, rng, low, top_value):
    shape = entries.shape
    place = [jax.random.randint(jax.random.fold_in(rng, axis), (), 0, shape[axis]) for axis in range(len(shape))]
    entries = entries.at[tuple(place)].set(low)
    longest = shape.index(max(shape))
    place[longest] = (place[longest] + 1) % shape[longest]
    return entries.at[tuple(place)].set(top_value)


def block_levels(own_key, shape, split, least, largest):
    def one(dim, parts):
        steps = jax.random.uniform(jax.random.fold_in(jax.random.fold_in(own_key, 6), dim), (parts,), jnp.float32, least / len(split), largest / len(split))
        return jnp.repeat(jnp.exp(steps), shape[dim] // parts).reshape((-1,) + (1,) * (len(shape) - dim - 1))

    factor_of = one(*split[0])
    for cut in split[1:]:
        factor_of = factor_of * one(*cut)
    return factor_of


def scatter_about(stream_key, shape, scale, reach, shards=(), held_as=jnp.bfloat16):
    values = scale * jax.random.normal(stream_key, shape, jnp.float32)
    if shards:
        values = values * block_levels(stream_key, shape, shards, -0.22, 0.18)
    return jnp.clip(values, -reach, reach).astype(held_as)


def setup_inputs(seed: int = 0) -> dict:
    streams_of = jax.random.split(jax.random.key(seed), 11)
    start_acts = scatter_about(streams_of[0], (SECTIONS, N_DP * ROWS, D), 1.0, 6.0, ((0, 32), (1, 2), (2, 8)))
    fresh_acts = scatter_about(streams_of[1], (TICKS - 1, N_DP * ROWS, D), 1.0, 6.0, ((1, 2), (2, 8)))
    ln_gain = jnp.clip(1.0 + 0.18 * jax.random.normal(streams_of[2], (SECTIONS, D), jnp.float32), 0.1, 1.9)
    ln_shift = scatter_about(streams_of[3], (SECTIONS, D), 0.3, 4.0, ((0, 32),), jnp.float32)
    proj = scatter_about(streams_of[4], (SECTIONS, D, D), D ** -0.5, 0.078125, ((0, 32), (1, 2), (2, 8)))
    proj_bias = scatter_about(streams_of[5], (SECTIONS, D), 0.5, 6.0, ((0, 32), (1, 8)), jnp.float32)
    sample_ids = place_ends(jax.random.randint(streams_of[6], (MICRO, N_DP * SEQS), 0, STORE), jax.random.fold_in(streams_of[6], 1), 0, STORE - 1).astype(jnp.int32)
    base_out = scatter_about(streams_of[7], (SECTIONS, N_DP * STORE, SEQLEN, D), 1.0, 6.0, ((0, 32), (1, 2), (3, 8)))
    base_in = scatter_about(streams_of[8], (SECTIONS, N_DP * STORE, SEQLEN, D), 1.0, 6.0, ((0, 32), (1, 2), (3, 8)))
    scale_exps = place_ends(jax.random.randint(streams_of[9], (SECTIONS, TICKS, N_DP * ROWS, NBLK), -1, 3), jax.random.fold_in(streams_of[9], 1), -1, 2).astype(jnp.int32)
    return dict(start_acts=start_acts, fresh_acts=fresh_acts, ln_gain=ln_gain, ln_shift=ln_shift, proj=proj, proj_bias=proj_bias, sample_ids=sample_ids, base_out=base_out, base_in=base_in, scale_exps=scale_exps)


norm_eps = 1e-05
clip_limit = 4.0

def normalize(values, gain_row, shift_row):
    average = lax.optimization_barrier(jnp.mean(values, axis=-1, keepdims=True))
    centered = values - average
    spread = lax.optimization_barrier(jnp.mean(centered * centered, axis=-1, keepdims=True))
    return (centered * lax.rsqrt(spread + norm_eps) * gain_row + shift_row).astype(jnp.bfloat16)

def block_factor(exponents):
    return jnp.repeat(jnp.exp2(exponents.astype(jnp.float32)), BLOCK, axis=-1)

def reference(start_acts, fresh_acts, ln_gain, ln_shift, proj, proj_bias, sample_ids, base_out, base_in, scale_exps):
    sections = start_acts.shape[0]
    micro = sample_ids.shape[0]
    width = start_acts.shape[2]
    seq_owner = jnp.arange(sample_ids.shape[1], dtype=jnp.int32) // SEQS * STORE
    section_ids = jnp.arange(sections, dtype=jnp.int32)

    def lookup(base_table, batch_index):
        ids_row = lax.dynamic_index_in_dim(sample_ids, batch_index, 0, keepdims=False)
        picked = jnp.take(base_table, (seq_owner + ids_row).astype(jnp.int32), axis=0)
        return picked.reshape(-1, width).astype(jnp.float32)
    current = start_acts
    outputs = []
    arrived = None
    for step_no in range(TICKS):

        def send(packed):
            section_id, acts, gain_row, shift_row, weight, bias_row, base_table, exponents = packed
            normed = normalize(acts.astype(jnp.float32), gain_row, shift_row)
            projected = jnp.dot(normed, weight, preferred_element_type=jnp.float32)
            result = (acts.astype(jnp.float32) + jax.nn.relu(projected + bias_row)).astype(jnp.bfloat16)
            batch_index = (step_no + sections - 1 - section_id).astype(jnp.int32)
            delta = result.astype(jnp.float32) - lookup(base_table, batch_index)
            coded = jnp.clip(delta / block_factor(exponents), -clip_limit, clip_limit).astype(jnp.bfloat16)
            return (result, coded)
        results, coded_all = lax.map(send, (section_ids, current, ln_gain, ln_shift, proj, proj_bias, base_out, scale_exps[:, step_no]))
        outputs.append(results)
        coded_prev = jnp.concatenate([jnp.zeros_like(coded_all[:1]), coded_all[:-1]], axis=0)
        exps_now = scale_exps[:, step_no]
        exps_prev = jnp.concatenate([exps_now[:1], exps_now[:-1]], axis=0)

        def receive(packed):
            section_id, base_table, coded, exponents = packed
            batch_index = jnp.minimum(step_no + sections - section_id, micro - 1).astype(jnp.int32)
            rebuilt = lookup(base_table, batch_index) + coded.astype(jnp.float32) * block_factor(exponents)
            return jnp.where(section_id > 0, rebuilt, jnp.zeros_like(rebuilt)).astype(jnp.bfloat16)
        arrived = lax.map(receive, (section_ids, base_in, coded_prev, exps_prev))
        if step_no + 1 < TICKS:
            current = arrived.at[0].set(fresh_acts[step_no])
    return (jnp.stack(outputs, axis=1), arrived)
```

```python
import functools

import jax
import jax.numpy as jnp
from jax import lax
from jax.experimental import pallas as pl
from jax.experimental.pallas import tpu as pltpu
from jax.sharding import PartitionSpec as P

TICKS = 3

norm_eps = 1e-05
clip_limit = 4.0
LANES = 128
VMEM_LIMIT = 16 * 1024 * 1024


def tick_kernel(
    step,
    ids,
    gathered,
    w_own,
    w_other,
    base_out,
    base_in,
    fresh,
    gain_far,
    shift_far,
    bias_far,
    exps_far,
    result,
    sent,
    held,
    normed,
    base,
    gain,
    shift,
    bias,
    exps,
    sem,
    load_sem,
):
    peers, rows, cols = gathered.shape
    seq = base_out.shape[1]
    seqs = rows // seq
    per_half = normed.shape[2] // cols
    tiles = [(peer, col) for peer in range(peers) for col in range(0, cols, LANES)]
    width = float(peers * cols)
    section = lax.axis_index("section")
    own = lax.axis_index("dp")
    mine = lax.axis_index("tensor")
    batch = step + lax.axis_size("section") - 1 - section
    arriving_batch = jnp.minimum(batch + 1, ids.shape[1] - 1)

    loads = [
        pltpu.make_async_copy(source, target, load_sem.at[load_no])
        for load_no, (source, target) in enumerate(
            [(gain_far, gain), (shift_far, shift), (bias_far, bias), (exps_far, exps)]
        )
    ]
    for load in loads:
        load.start()
    bases = []
    for seq_no in range(seqs):
        low = seq_no * seq
        place = pl.ds(low, seq)
        bases.append(
            pltpu.make_async_copy(
                base_out.at[ids[seq_no, batch]], base.at[place], sem.at[seq_no]
            )
        )
        bases[-1].start()
        in_slot = ids[seq_no, arriving_batch]

        @pl.when(section > 0)
        def _():
            pltpu.make_async_copy(
                base_in.at[in_slot], held.at[place], sem.at[seqs + seq_no]
            ).start()

        if step < fresh.shape[0]:

            @pl.when(section == 0)
            def _():
                pltpu.make_async_copy(
                    fresh.at[step, place], held.at[place], sem.at[seqs + seq_no]
                ).start()

    total = jnp.zeros((rows, LANES), jnp.float32)
    for peer, col in tiles:
        total += gathered[peer, :, col : col + LANES].astype(jnp.float32)
    average = jnp.sum(total, axis=-1, keepdims=True) / width
    total = jnp.zeros((rows, LANES), jnp.float32)
    for peer, col in tiles:
        centered = gathered[peer, :, col : col + LANES].astype(jnp.float32) - average
        total += centered * centered
    scale = lax.rsqrt(jnp.sum(total, axis=-1, keepdims=True) / width + norm_eps)
    for load in loads:
        load.wait()
    for peer, col in tiles:
        at = peer * cols + col
        centered = gathered[peer, :, col : col + LANES].astype(jnp.float32) - average
        value = centered * scale * gain[:, at : at + LANES] + shift[:, at : at + LANES]
        start = (peer % per_half) * cols + col
        normed[peer // per_half, :, start : start + LANES] = value.astype(jnp.bfloat16)

    projected = jnp.dot(normed[own], w_own[...], preferred_element_type=jnp.float32)
    projected += jnp.dot(normed[1 - own], w_other[...], preferred_element_type=jnp.float32)
    relu = jnp.maximum(projected + bias[...], 0.0)
    result[...] = (gathered[mine].astype(jnp.float32) + relu).astype(jnp.bfloat16)
    for copy in bases:
        copy.wait()
    for block in range(cols // LANES):
        top = clip_limit * jnp.exp2(exps[step, block].astype(jnp.float32))
        top = jnp.transpose(jnp.broadcast_to(top, (LANES, rows)))
        span = slice(block * LANES, (block + 1) * LANES)
        delta = result[:, span].astype(jnp.float32) - base[:, span].astype(jnp.float32)
        sent[:, span] = jnp.clip(delta, -top, top).astype(jnp.bfloat16)
    for seq_no in range(seqs):
        landed = pltpu.make_async_copy(
            base_in.at[0], held.at[pl.ds(seq_no * seq, seq)], sem.at[seqs + seq_no]
        )
        if step < fresh.shape[0]:
            landed.wait()
        else:

            @pl.when(section > 0)
            def _():
                landed.wait()

            @pl.when(section == 0)
            def _():
                held[seq_no * seq : (seq_no + 1) * seq] = jnp.zeros((seq, cols), jnp.bfloat16)


def copies_kernel(source, copies, held, sem):
    load = pltpu.make_async_copy(source, held, sem)
    load.start()
    load.wait()
    for peer in range(copies.shape[0]):
        copies[peer] = held[...]


def rebuild_kernel(held, arriving, copies):
    total = held[...].astype(jnp.float32) + arriving[...].astype(jnp.float32)
    rebuilt = total.astype(jnp.bfloat16)
    for peer in range(copies.shape[0]):
        copies[peer] = rebuilt


VMEM = pl.BlockSpec(memory_space=pltpu.VMEM)
SMEM = pl.BlockSpec(memory_space=pltpu.SMEM)
HBM = pl.BlockSpec(memory_space=pltpu.HBM)


def in_hbm(*arrays):
    return [pltpu.with_memory_space_constraint(array, pltpu.HBM) for array in arrays]


def tick(step, ids, gathered, gain, shift, bias, w_own, w_other, base_out, base_in, fresh, exps):
    peers, rows, cols = gathered.shape
    depth = w_own.shape[0]
    seqs = rows // base_out.shape[1]
    out = jax.ShapeDtypeStruct((rows, cols), jnp.bfloat16)
    return pl.pallas_call(
        functools.partial(tick_kernel, step),
        out_shape=(out, out, out),
        in_specs=[SMEM] + [VMEM] * 3 + [HBM] * 7,
        out_specs=(VMEM,) * 3,
        scratch_shapes=[
            pltpu.VMEM((2, rows, depth), jnp.bfloat16),
            pltpu.VMEM((rows, cols), jnp.bfloat16),
            pltpu.VMEM(gain.shape, jnp.float32),
            pltpu.VMEM(shift.shape, jnp.float32),
            pltpu.VMEM(bias.shape, jnp.float32),
            pltpu.VMEM(exps.shape, jnp.int32),
            pltpu.SemaphoreType.DMA((2 * seqs,)),
            pltpu.SemaphoreType.DMA((4,)),
        ],
        compiler_params=pltpu.CompilerParams(vmem_limit_bytes=VMEM_LIMIT),
        cost_estimate=pl.CostEstimate(
            flops=4 * rows * depth * cols, bytes_accessed=4 * depth * cols, transcendentals=0
        ),
        name="tick",
    )(ids, gathered, w_own, w_other, *in_hbm(base_out, base_in, fresh, gain, shift, bias, exps))


def copies_of(block, peers):
    rows, cols = block.shape
    return pl.pallas_call(
        copies_kernel,
        out_shape=jax.ShapeDtypeStruct((peers, rows, cols), jnp.bfloat16),
        in_specs=[HBM],
        out_specs=VMEM,
        scratch_shapes=[pltpu.VMEM((rows, cols), jnp.bfloat16), pltpu.SemaphoreType.DMA(())],
        compiler_params=pltpu.CompilerParams(vmem_limit_bytes=VMEM_LIMIT),
        cost_estimate=pl.CostEstimate(
            flops=0, bytes_accessed=2 * (peers + 1) * rows * cols, transcendentals=0
        ),
        name="copies",
    )(*in_hbm(block))


def rebuild(peers, held, arriving):
    rows, cols = arriving.shape
    return pl.pallas_call(
        rebuild_kernel,
        out_shape=jax.ShapeDtypeStruct((peers, rows, cols), jnp.bfloat16),
        in_specs=[VMEM, VMEM],
        out_specs=VMEM,
        compiler_params=pltpu.CompilerParams(vmem_limit_bytes=VMEM_LIMIT),
        cost_estimate=pl.CostEstimate(
            flops=2 * rows * cols, bytes_accessed=2 * (peers + 2) * rows * cols, transcendentals=0
        ),
        name="rebuild",
    )(held, arriving)


def shards(
    start_acts,
    fresh_acts,
    ln_gain,
    ln_shift,
    proj,
    proj_bias,
    sample_ids,
    base_out,
    base_in,
    scale_exps,
):
    sections = lax.axis_size("section")
    peers = lax.axis_size("tensor")
    forward = [(source, source + 1) for source in range(sections - 1)]
    w_own = proj[0]
    w_other = lax.ppermute(w_own, "dp", [(0, 1), (1, 0)])
    ids = jnp.transpose(sample_ids)
    exps = jnp.transpose(scale_exps, (1, 3, 0, 2))
    copies = copies_of(start_acts[0], peers)
    outputs = []
    for step in range(TICKS):
        gathered = lax.all_to_all(copies, "tensor", 0, 0)
        result, sent, held = tick(
            step, ids, gathered, ln_gain, ln_shift, proj_bias, w_own, w_other, base_out[0], base_in[0],
            fresh_acts, exps,
        )
        outputs.append(result)
        arriving = lax.ppermute(sent, "section", forward)
        copies = rebuild(peers if step + 1 < TICKS else 1, held, arriving)
    return (jnp.stack(outputs, axis=0)[None], copies)


def solution(mesh):
    return jax.shard_map(
        shards,
        mesh=mesh,
        in_specs=(
            P("section", "dp", "tensor"),
            P(None, "dp", "tensor"),
            P("section", None),
            P("section", None),
            P("section", "dp", "tensor"),
            P("section", "tensor"),
            P(None, "dp"),
            P("section", "dp", None, "tensor"),
            P("section", "dp", None, "tensor"),
            P("section", None, "dp", "tensor"),
        ),
        out_specs=(P("section", None, "dp", "tensor"), P("section", "dp", "tensor")),
        check_vma=False,
    )
```

```python
import functools

import jax
import jax.numpy as jnp
from jax import lax
from jax.experimental import pallas as pl
from jax.experimental.pallas import tpu as pltpu
from jax.sharding import PartitionSpec as P

TICKS = 3

norm_eps = 1e-05
clip_limit = 4.0
LANES = 128
VMEM_LIMIT = 16 * 1024 * 1024


def tick_kernel(
    step,
    ids,
    gathered,
    w_own,
    w_other,
    base_out,
    base_in,
    fresh,
    gain_far,
    shift_far,
    bias_far,
    exps_far,
    result,
    sent,
    held,
    normed,
    projected,
    base,
    gain,
    shift,
    bias,
    exps,
    sem,
    load_sem,
):
    peers, rows, cols = gathered.shape
    seq = base_out.shape[1]
    seqs = rows // seq
    per_half = normed.shape[2] // cols
    tiles = [(peer, col) for peer in range(peers) for col in range(0, cols, LANES)]
    width = float(peers * cols)
    section = lax.axis_index("section")
    own = lax.axis_index("dp")
    mine = lax.axis_index("tensor")
    batch = step + lax.axis_size("section") - 1 - section
    arriving_batch = jnp.minimum(batch + 1, ids.shape[1] - 1)

    loads = [
        pltpu.make_async_copy(source, target, load_sem.at[load_no])
        for load_no, (source, target) in enumerate(
            [(gain_far, gain), (shift_far, shift), (bias_far, bias), (exps_far, exps)]
        )
    ]
    for load in loads:
        load.start()
    bases = []
    for seq_no in range(seqs):
        low = seq_no * seq
        place = pl.ds(low, seq)
        bases.append(
            pltpu.make_async_copy(
                base_out.at[ids[seq_no, batch]], base.at[place], sem.at[seq_no]
            )
        )
        bases[-1].start()
        in_slot = ids[seq_no, arriving_batch]

        @pl.when(section > 0)
        def _():
            pltpu.make_async_copy(
                base_in.at[in_slot], held.at[place], sem.at[seqs + seq_no]
            ).start()

        if step < fresh.shape[0]:

            @pl.when(section == 0)
            def _():
                pltpu.make_async_copy(
                    fresh.at[step, place], held.at[place], sem.at[seqs + seq_no]
                ).start()

    total = jnp.zeros((rows, LANES), jnp.float32)
    for peer, col in tiles:
        total += gathered[peer, :, col : col + LANES].astype(jnp.float32)
    average = jnp.sum(total, axis=-1, keepdims=True) / width
    total = jnp.zeros((rows, LANES), jnp.float32)
    for peer, col in tiles:
        centered = gathered[peer, :, col : col + LANES].astype(jnp.float32) - average
        total += centered * centered
    scale = lax.rsqrt(jnp.sum(total, axis=-1, keepdims=True) / width + norm_eps)
    for load in loads:
        load.wait()

    def norm_half(half):
        for peer, col in tiles[half * len(tiles) // 2 : (half + 1) * len(tiles) // 2]:
            at = peer * cols + col
            centered = gathered[peer, :, col : col + LANES].astype(jnp.float32) - average
            value = centered * scale * gain[:, at : at + LANES] + shift[:, at : at + LANES]
            start = (peer % per_half) * cols + col
            normed[half, :, start : start + LANES] = value.astype(jnp.bfloat16)

    def project(first, second):
        norm_half(0)
        low = jnp.dot(normed[0], first[...], preferred_element_type=jnp.float32)
        norm_half(1)
        high = jnp.dot(normed[1], second[...], preferred_element_type=jnp.float32)
        projected[...] = low + high + bias[...]

    @pl.when(own == 0)
    def _():
        project(w_own, w_other)

    @pl.when(own != 0)
    def _():
        project(w_other, w_own)

    relu = jnp.maximum(projected[...], 0.0)
    result[...] = (gathered[mine].astype(jnp.float32) + relu).astype(jnp.bfloat16)
    for copy in bases:
        copy.wait()
    for block in range(cols // LANES):
        top = clip_limit * jnp.exp2(exps[step, block].astype(jnp.float32))
        top = jnp.transpose(jnp.broadcast_to(top, (LANES, rows)))
        span = slice(block * LANES, (block + 1) * LANES)
        delta = result[:, span].astype(jnp.float32) - base[:, span].astype(jnp.float32)
        sent[:, span] = jnp.clip(delta, -top, top).astype(jnp.bfloat16)
    for seq_no in range(seqs):
        landed = pltpu.make_async_copy(
            base_in.at[0], held.at[pl.ds(seq_no * seq, seq)], sem.at[seqs + seq_no]
        )
        if step < fresh.shape[0]:
            landed.wait()
        else:

            @pl.when(section > 0)
            def _():
                landed.wait()

            @pl.when(section == 0)
            def _():
                held[seq_no * seq : (seq_no + 1) * seq] = jnp.zeros((seq, cols), jnp.bfloat16)


def copies_kernel(source, copies):
    block = source[...]
    for peer in range(copies.shape[0]):
        copies[peer] = block


def rebuild_kernel(held, arriving, copies):
    total = held[...].astype(jnp.float32) + arriving[...].astype(jnp.float32)
    rebuilt = total.astype(jnp.bfloat16)
    for peer in range(copies.shape[0]):
        copies[peer] = rebuilt


VMEM = pl.BlockSpec(memory_space=pltpu.VMEM)
SMEM = pl.BlockSpec(memory_space=pltpu.SMEM)
HBM = pl.BlockSpec(memory_space=pltpu.HBM)


def in_hbm(*arrays):
    return [pltpu.with_memory_space_constraint(array, pltpu.HBM) for array in arrays]


def tick(step, ids, gathered, gain, shift, bias, w_own, w_other, base_out, base_in, fresh, exps):
    peers, rows, cols = gathered.shape
    depth = w_own.shape[0]
    seqs = rows // base_out.shape[1]
    out = jax.ShapeDtypeStruct((rows, cols), jnp.bfloat16)
    return pl.pallas_call(
        functools.partial(tick_kernel, step),
        out_shape=(out, out, out),
        in_specs=[SMEM] + [VMEM] * 3 + [HBM] * 7,
        out_specs=(VMEM,) * 3,
        scratch_shapes=[
            pltpu.VMEM((2, rows, depth), jnp.bfloat16),
            pltpu.VMEM((rows, cols), jnp.float32),
            pltpu.VMEM((rows, cols), jnp.bfloat16),
            pltpu.VMEM(gain.shape, jnp.float32),
            pltpu.VMEM(shift.shape, jnp.float32),
            pltpu.VMEM(bias.shape, jnp.float32),
            pltpu.VMEM(exps.shape, jnp.int32),
            pltpu.SemaphoreType.DMA((2 * seqs,)),
            pltpu.SemaphoreType.DMA((4,)),
        ],
        compiler_params=pltpu.CompilerParams(vmem_limit_bytes=VMEM_LIMIT),
        cost_estimate=pl.CostEstimate(
            flops=4 * rows * depth * cols, bytes_accessed=4 * depth * cols, transcendentals=0
        ),
        name="tick",
    )(ids, gathered, w_own, w_other, *in_hbm(base_out, base_in, fresh, gain, shift, bias, exps))


def copies_of(block, peers):
    rows, cols = block.shape
    return pl.pallas_call(
        copies_kernel,
        out_shape=jax.ShapeDtypeStruct((peers, rows, cols), jnp.bfloat16),
        in_specs=[VMEM],
        out_specs=VMEM,
        compiler_params=pltpu.CompilerParams(vmem_limit_bytes=VMEM_LIMIT),
        cost_estimate=pl.CostEstimate(
            flops=0, bytes_accessed=2 * (peers + 1) * rows * cols, transcendentals=0
        ),
        name="copies",
    )(block)


def rebuild(peers, held, arriving):
    rows, cols = arriving.shape
    return pl.pallas_call(
        rebuild_kernel,
        out_shape=jax.ShapeDtypeStruct((peers, rows, cols), jnp.bfloat16),
        in_specs=[VMEM, VMEM],
        out_specs=VMEM,
        compiler_params=pltpu.CompilerParams(vmem_limit_bytes=VMEM_LIMIT),
        cost_estimate=pl.CostEstimate(
            flops=2 * rows * cols, bytes_accessed=2 * (peers + 2) * rows * cols, transcendentals=0
        ),
        name="rebuild",
    )(held, arriving)


def shards(
    start_acts,
    fresh_acts,
    ln_gain,
    ln_shift,
    proj,
    proj_bias,
    sample_ids,
    base_out,
    base_in,
    scale_exps,
):
    sections = lax.axis_size("section")
    peers = lax.axis_size("tensor")
    forward = [(source, source + 1) for source in range(sections - 1)]
    w_own = proj[0]
    w_other = lax.ppermute(w_own, "dp", [(0, 1), (1, 0)])
    ids = jnp.transpose(sample_ids)
    exps = jnp.transpose(scale_exps, (1, 3, 0, 2))
    copies = copies_of(start_acts[0], peers)
    outputs = []
    for step in range(TICKS):
        gathered = lax.all_to_all(copies, "tensor", 0, 0)
        result, sent, held = tick(
            step, ids, gathered, ln_gain, ln_shift, proj_bias, w_own, w_other, base_out[0], base_in[0],
            fresh_acts, exps,
        )
        outputs.append(result)
        arriving = lax.ppermute(sent, "section", forward)
        copies = rebuild(peers if step + 1 < TICKS else 1, held, arriving)
    return (jnp.stack(outputs, axis=0)[None], copies)


def solution(mesh):
    return jax.shard_map(
        shards,
        mesh=mesh,
        in_specs=(
            P("section", "dp", "tensor"),
            P(None, "dp", "tensor"),
            P("section", None),
            P("section", None),
            P("section", "dp", "tensor"),
            P("section", "tensor"),
            P(None, "dp"),
            P("section", "dp", None, "tensor"),
            P("section", "dp", None, "tensor"),
            P("section", None, "dp", "tensor"),
        ),
        out_specs=(P("section", None, "dp", "tensor"), P("section", "dp", "tensor")),
        check_vma=False,
    )
```

```python
import functools

import jax
import jax.numpy as jnp
from jax import lax
from jax.experimental import pallas as pl
from jax.experimental.pallas import tpu as pltpu
from jax.sharding import PartitionSpec as P

TICKS = 3

norm_eps = 1e-05
clip_limit = 4.0
LANES = 128
VMEM_LIMIT = 16 * 1024 * 1024


def tick_kernel(
    step,
    ids,
    gathered,
    w_own,
    w_other,
    base_out,
    base_in,
    fresh,
    gain_far,
    shift_far,
    bias_far,
    exps_far,
    result,
    sent,
    held,
    normed,
    projected,
    base,
    gain,
    shift,
    bias,
    exps,
    sem,
    load_sem,
):
    peers, rows, cols = gathered.shape
    seq = base_out.shape[1]
    seqs = rows // seq
    per_half = normed.shape[2] // cols
    tiles = [(peer, col) for peer in range(peers) for col in range(0, cols, LANES)]
    width = float(peers * cols)
    section = lax.axis_index("section")
    own = lax.axis_index("dp")
    mine = lax.axis_index("tensor")
    batch = step + lax.axis_size("section") - 1 - section
    arriving_batch = jnp.minimum(batch + 1, ids.shape[1] - 1)

    loads = [
        pltpu.make_async_copy(source, target, load_sem.at[load_no])
        for load_no, (source, target) in enumerate(
            [(gain_far, gain), (shift_far, shift), (bias_far, bias), (exps_far, exps)]
        )
    ]
    for load in loads:
        load.start()
    bases = []
    for seq_no in range(seqs):
        low = seq_no * seq
        place = pl.ds(low, seq)
        bases.append(
            pltpu.make_async_copy(
                base_out.at[ids[seq_no, batch]], base.at[place], sem.at[seq_no]
            )
        )
        bases[-1].start()
        in_slot = ids[seq_no, arriving_batch]

        @pl.when(section > 0)
        def _():
            pltpu.make_async_copy(
                base_in.at[in_slot], held.at[place], sem.at[seqs + seq_no]
            ).start()

        if step < fresh.shape[0]:

            @pl.when(section == 0)
            def _():
                pltpu.make_async_copy(
                    fresh.at[step, place], held.at[place], sem.at[seqs + seq_no]
                ).start()

    near = gathered[0, :, :1].astype(jnp.float32)
    total = jnp.zeros((rows, LANES), jnp.float32)
    squares = jnp.zeros((rows, LANES), jnp.float32)
    for peer, col in tiles:
        offset = gathered[peer, :, col : col + LANES].astype(jnp.float32) - near
        total += offset
        squares += offset * offset
    shifted = jnp.sum(total, axis=-1, keepdims=True) / width
    spread = jnp.sum(squares, axis=-1, keepdims=True) / width - shifted * shifted
    average = near + shifted
    scale = lax.rsqrt(jnp.maximum(spread, 0.0) + norm_eps)
    for load in loads:
        load.wait()

    def norm_half(half):
        for peer, col in tiles[half * len(tiles) // 2 : (half + 1) * len(tiles) // 2]:
            at = peer * cols + col
            centered = gathered[peer, :, col : col + LANES].astype(jnp.float32) - average
            value = centered * scale * gain[:, at : at + LANES] + shift[:, at : at + LANES]
            start = (peer % per_half) * cols + col
            normed[half, :, start : start + LANES] = value.astype(jnp.bfloat16)

    def project(first, second):
        norm_half(0)
        low = jnp.dot(normed[0], first[...], preferred_element_type=jnp.float32)
        norm_half(1)
        high = jnp.dot(normed[1], second[...], preferred_element_type=jnp.float32)
        projected[...] = low + high + bias[...]

    @pl.when(own == 0)
    def _():
        project(w_own, w_other)

    @pl.when(own != 0)
    def _():
        project(w_other, w_own)

    relu = jnp.maximum(projected[...], 0.0)
    result[...] = (gathered[mine].astype(jnp.float32) + relu).astype(jnp.bfloat16)
    for copy in bases:
        copy.wait()
    for block in range(cols // LANES):
        top = clip_limit * jnp.exp2(exps[step, block].astype(jnp.float32))
        top = jnp.transpose(jnp.broadcast_to(top, (LANES, rows)))
        span = slice(block * LANES, (block + 1) * LANES)
        delta = result[:, span].astype(jnp.float32) - base[:, span].astype(jnp.float32)
        sent[:, span] = jnp.clip(delta, -top, top).astype(jnp.bfloat16)
    for seq_no in range(seqs):
        landed = pltpu.make_async_copy(
            base_in.at[0], held.at[pl.ds(seq_no * seq, seq)], sem.at[seqs + seq_no]
        )
        if step < fresh.shape[0]:
            landed.wait()
        else:

            @pl.when(section > 0)
            def _():
                landed.wait()

            @pl.when(section == 0)
            def _():
                held[seq_no * seq : (seq_no + 1) * seq] = jnp.zeros((seq, cols), jnp.bfloat16)


def copies_kernel(source, copies):
    block = source[...]
    for peer in range(copies.shape[0]):
        copies[peer] = block


def rebuild_kernel(held, arriving, copies):
    total = held[...].astype(jnp.float32) + arriving[...].astype(jnp.float32)
    rebuilt = total.astype(jnp.bfloat16)
    for peer in range(copies.shape[0]):
        copies[peer] = rebuilt


VMEM = pl.BlockSpec(memory_space=pltpu.VMEM)
SMEM = pl.BlockSpec(memory_space=pltpu.SMEM)
HBM = pl.BlockSpec(memory_space=pltpu.HBM)


def in_hbm(*arrays):
    return [pltpu.with_memory_space_constraint(array, pltpu.HBM) for array in arrays]


def tick(step, ids, gathered, gain, shift, bias, w_own, w_other, base_out, base_in, fresh, exps):
    peers, rows, cols = gathered.shape
    depth = w_own.shape[0]
    seqs = rows // base_out.shape[1]
    out = jax.ShapeDtypeStruct((rows, cols), jnp.bfloat16)
    return pl.pallas_call(
        functools.partial(tick_kernel, step),
        out_shape=(out, out, out),
        in_specs=[SMEM] + [VMEM] * 3 + [HBM] * 7,
        out_specs=(VMEM,) * 3,
        scratch_shapes=[
            pltpu.VMEM((2, rows, depth), jnp.bfloat16),
            pltpu.VMEM((rows, cols), jnp.float32),
            pltpu.VMEM((rows, cols), jnp.bfloat16),
            pltpu.VMEM(gain.shape, jnp.float32),
            pltpu.VMEM(shift.shape, jnp.float32),
            pltpu.VMEM(bias.shape, jnp.float32),
            pltpu.VMEM(exps.shape, jnp.int32),
            pltpu.SemaphoreType.DMA((2 * seqs,)),
            pltpu.SemaphoreType.DMA((4,)),
        ],
        compiler_params=pltpu.CompilerParams(vmem_limit_bytes=VMEM_LIMIT),
        cost_estimate=pl.CostEstimate(
            flops=4 * rows * depth * cols, bytes_accessed=4 * depth * cols, transcendentals=0
        ),
        name="tick",
    )(ids, gathered, w_own, w_other, *in_hbm(base_out, base_in, fresh, gain, shift, bias, exps))


def copies_of(block, peers):
    rows, cols = block.shape
    return pl.pallas_call(
        copies_kernel,
        out_shape=jax.ShapeDtypeStruct((peers, rows, cols), jnp.bfloat16),
        in_specs=[VMEM],
        out_specs=VMEM,
        compiler_params=pltpu.CompilerParams(vmem_limit_bytes=VMEM_LIMIT),
        cost_estimate=pl.CostEstimate(
            flops=0, bytes_accessed=2 * (peers + 1) * rows * cols, transcendentals=0
        ),
        name="copies",
    )(block)


def rebuild(peers, held, arriving):
    rows, cols = arriving.shape
    return pl.pallas_call(
        rebuild_kernel,
        out_shape=jax.ShapeDtypeStruct((peers, rows, cols), jnp.bfloat16),
        in_specs=[VMEM, VMEM],
        out_specs=VMEM,
        compiler_params=pltpu.CompilerParams(vmem_limit_bytes=VMEM_LIMIT),
        cost_estimate=pl.CostEstimate(
            flops=2 * rows * cols, bytes_accessed=2 * (peers + 2) * rows * cols, transcendentals=0
        ),
        name="rebuild",
    )(held, arriving)


def shards(
    start_acts,
    fresh_acts,
    ln_gain,
    ln_shift,
    proj,
    proj_bias,
    sample_ids,
    base_out,
    base_in,
    scale_exps,
):
    sections = lax.axis_size("section")
    peers = lax.axis_size("tensor")
    forward = [(source, source + 1) for source in range(sections - 1)]
    w_own = proj[0]
    w_other = lax.ppermute(w_own, "dp", [(0, 1), (1, 0)])
    ids = jnp.transpose(sample_ids)
    exps = jnp.transpose(scale_exps, (1, 3, 0, 2))
    copies = copies_of(start_acts[0], peers)
    outputs = []
    for step in range(TICKS):
        gathered = lax.all_to_all(copies, "tensor", 0, 0)
        result, sent, held = tick(
            step, ids, gathered, ln_gain, ln_shift, proj_bias, w_own, w_other, base_out[0], base_in[0],
            fresh_acts, exps,
        )
        outputs.append(result)
        arriving = lax.ppermute(sent, "section", forward)
        copies = rebuild(peers if step + 1 < TICKS else 1, held, arriving)
    return (jnp.stack(outputs, axis=0)[None], copies)


def solution(mesh):
    return jax.shard_map(
        shards,
        mesh=mesh,
        in_specs=(
            P("section", "dp", "tensor"),
            P(None, "dp", "tensor"),
            P("section", None),
            P("section", None),
            P("section", "dp", "tensor"),
            P("section", "tensor"),
            P(None, "dp"),
            P("section", "dp", None, "tensor"),
            P("section", "dp", None, "tensor"),
            P("section", None, "dp", "tensor"),
        ),
        out_specs=(P("section", None, "dp", "tensor"), P("section", "dp", "tensor")),
        check_vma=False,
    )
```
